32 devices in a mesh: shard: 2 (over y), row: 16 (over z, x, core).
Axes of the slice: x: 2, y: 2, z: 4, core: 2. Of those that a mesh axis runs over, the one named last changes fastest.
Arguments:
- documents: bfloat16 [32768, 4096], P(('shard', 'row')), parts along dimension 0, may hold values from -60 to 60
- queries: bfloat16 [128, 4096], P('row'), may hold values from -6 to 6
- precond: bfloat16 [4, 1024, 1024], P(None, 'row'), may hold values from -1 to 3, as said below
Outputs:
- scores: float32 [32768, 128], P(('shard', 'row')), parts along dimension 0
The draws below stay inside these ranges and needn't reach their ends.
There are 2 independent parts, one for each index of `shard`. The reference program is written for one: setup_inputs(seed, part) draws one part's arguments, and reference() takes and returns one part's arrays. A program takes and returns all parts, laid end to end along the dimension named above; an argument that names none is the same for every part. Nothing has to cross between parts.
Inputs may be any that keep to these rules, and one draw needn't show every extreme that they name: Each block precond[b] is symmetric with a positive diagonal.
All inputs are finite; a program needn't handle non-finite values.
Results may differ from the reference program's by a relative error of at most 0.0029.
Values may be sent and summed in bfloat16 or wider, within the bound.
No kernel may reach another device: no remote copies, remote signals or barrier semaphores. Data moves between devices by JAX's collectives and lax.ppermute only.
A program may use at most 64 MiB of HBM per device.

```python
import jax
import jax.numpy as jnp
from jax import lax

PANELS = 4
PW = 1024
K = 4096
DOC_DEV = 1024
DOCS = 16384
QUERIES = 128
N_ROW = 16


def draw_documents(key, part):
    key = jax.random.fold_in(key, 1)
    key_main, key_rows, key_cols = jax.random.split(key, 3)
    base = jax.random.truncated_normal(key_main, -4.0, 4.0, (DOCS, K), jnp.float32)
    lo = 0.3
    hi = 3.0
    rows = jnp.exp(jax.random.uniform(key_rows, (DOCS, 1), jnp.float32, jnp.log(lo), jnp.log(hi)))
    cols = jnp.exp(jax.random.uniform(key_cols, (1, K), jnp.float32, jnp.log(0.5), jnp.log(2.0)))
    return (base * rows * cols).astype(jnp.bfloat16)


def draw_precond(key, part):
    key = jax.random.fold_in(key, 2)
    key_off, key_diag = jax.random.split(key)
    noise = jax.random.truncated_normal(key_off, -4.0, 4.0, (PANELS, PW, PW), jnp.float32)
    noise = noise * (0.5 / jnp.sqrt(jnp.float32(PW)))
    symmetric = (noise + jnp.swapaxes(noise, 1, 2)) * 0.7071
    diag_values = jnp.exp(jax.random.uniform(key_diag, (PANELS, PW, 1), jnp.float32, jnp.log(0.5), jnp.log(2.0)))
    positions = jnp.arange(PW)
    identity = (positions[:, None] == positions[None, :]).astype(jnp.float32)
    return (symmetric * (1.0 - identity) + identity[None, :, :] * diag_values).astype(jnp.bfloat16)


def block_levels(key, shape, cuts, least, largest):
    def one(axis_at, shards_of):
        heights = jax.random.uniform(jax.random.fold_in(jax.random.fold_in(key, 6), axis_at), (shards_of,), jnp.float32, least / len(cuts), largest / len(cuts))
        return jnp.repeat(jnp.exp(heights), shape[axis_at] // shards_of).reshape((-1,) + (1,) * (len(shape) - axis_at - 1))

    loudness = one(*cuts[0])
    for cut in cuts[1:]:
        loudness = loudness * one(*cut)
    return loudness


def bell_draw(own_key, shape, scale, bound, cuts=(), held_as=jnp.bfloat16):
    level = block_levels(own_key, shape, cuts, -0.22, 0.18) if cuts else 1.0
    array = jax.random.normal(own_key, shape, jnp.float32) * scale * level
    return jnp.minimum(jnp.maximum(array, -bound), bound).astype(held_as)


def setup_inputs(seed: int = 0, part: int = 0) -> dict:
    streams_of = jax.random.split(jax.random.key(seed), 4)
    part_splits = jax.random.split(jax.random.fold_in(streams_of[3], part), 4)
    return {
        "documents": draw_documents(jax.random.fold_in(jax.random.fold_in(streams_of[3], part), 71), part),
        "queries": bell_draw(streams_of[1], (QUERIES, K), 1.0, 6.0, ((0, 16),)),
        "precond": draw_precond(jax.random.fold_in(streams_of[3], 71), part),
    }


def reference(documents, queries, precond):
    qpanels = queries.astype(jnp.float32).reshape(QUERIES, PANELS, PW)
    pmat = precond.astype(jnp.float32)
    conditioned = jnp.einsum('qbk,brk->qbr', qpanels, pmat, precision=lax.Precision.HIGHEST)
    conditioned = conditioned.astype(jnp.bfloat16).reshape(QUERIES, K)
    blocks = documents.reshape(N_ROW, DOC_DEV, K)

    def one_block(block):
        raw = jnp.dot(block, conditioned.T, preferred_element_type=jnp.float32)
        dense = block.astype(jnp.float32)
        spread = jnp.sqrt(lax.optimization_barrier(jnp.mean(dense * dense, axis=1)) + 1e-06)
        return raw / (spread[:, None] * jnp.sqrt(jnp.float32(K)))
    return lax.map(one_block, blocks).reshape(DOCS, QUERIES)
```

```python
import functools

import jax
import jax.numpy as jnp
from jax import lax
from jax.experimental import pallas as pl
from jax.experimental.pallas import tpu as pltpu
from jax.sharding import PartitionSpec as P

AXES = ("shard", "row")
F32, BF16 = jnp.float32, jnp.bfloat16
VMEM_BYTES = 48 * 1024 * 1024


def place():
    row = lax.axis_index("row")
    return lax.axis_index("shard"), row // 4, (row // 2) % 2, row % 2


def swap(array, dy=0, dz=0, dx=0, dc=0, shear=False, only=None):
    pairs = []
    for y in range(2):
        for z in range(4):
            for x in range(2):
                for c in range(2):
                    sx = x ^ dx ^ (y if shear else 0)
                    source = (y ^ dy) * 16 + (z ^ dz) * 4 + sx * 2 + (c ^ dc)
                    pairs.append((source, y * 16 + z * 4 + x * 2 + c))
    return lax.ppermute(array, AXES, pairs)


def condition_kernel(q0, q1, q2, q3, own, other, out, acc):
    _, z, _, c = place()
    panels, rows, width = own.shape
    for b in range(panels):
        at = slice(b * width, (b + 1) * width)
        asked = jnp.concatenate([q[:, at].astype(F32) for q in (q0, q1, q2, q3)], axis=0)
        block = jnp.concatenate([own[b], other[b]], axis=0)
        got = lax.dot_general(
            asked.astype(BF16), block, (((1,), (1,)), ((), ())), preferred_element_type=F32
        )
        got = pltpu.roll(got, c * rows, axis=1)
        for k in range(4):
            acc[pl.ds(pl.multiple_of((z ^ k) * 8, 8), 8), b * 128 : (b + 1) * 128] = got[
                k * 8 : (k + 1) * 8
            ]
    out[...] = acc[...].astype(BF16)


def score_kernel(order, docs, *refs):
    pieces, (out, held, ready) = refs[: len(order)], refs[len(order) :]
    y, z, x, c = place()
    width = docs.shape[1]

    @pl.when(pl.program_id(0) == 0)
    def _():
        for (dy, dx, dc), piece in zip(order, pieces, strict=True):
            px = x ^ dx
            slot = (px ^ y ^ dy) * 2 + (c ^ dc)
            rows = pl.ds(pl.multiple_of(slot * 32, 32), 32)
            for k in range(4):
                for b in range(4):
                    start = b * (width // 4) + (z ^ k) * 256 + px * 128
                    held[rows, pl.ds(pl.multiple_of(start, 128), 128)] = piece[
                        k, :, b * 128 : (b + 1) * 128
                    ]
        step = 512
        for at in range(0, width, step):
            part = held[:, at : at + step].astype(F32).reshape(4, 4, 8, step)
            part = jnp.concatenate(
                [part[s, k] for k in range(4) for s in range(4)], axis=0
            )
            ready[:, at : at + step] = part.astype(BF16)

    block = docs[...]
    raw = lax.dot_general(
        block, ready[...], (((1,), (1,)), ((), ())), preferred_element_type=F32
    )
    dense = block.astype(F32)
    mean = jnp.sum(dense * dense, axis=1, keepdims=True) * (1.0 / width)
    out[...] = raw * (lax.rsqrt(mean + 1e-06) * (1.0 / width**0.5))


def grouped(documents, queries, precond):
    doc_count, width = documents.shape
    q3 = swap(queries, dz=3, shear=True)
    q2 = swap(queries, dz=2, shear=True)
    q1 = swap(queries, dz=1, shear=True)
    q0 = swap(queries, dz=0, shear=True)
    other = swap(precond, dc=1)
    vmem = pl.BlockSpec(memory_space=pltpu.VMEM)
    piece = pl.pallas_call(
        condition_kernel,
        out_shape=jax.ShapeDtypeStruct((32, 512), BF16),
        in_specs=[vmem] * 6,
        out_specs=vmem,
        scratch_shapes=[pltpu.VMEM((32, 512), F32)],
        compiler_params=pltpu.CompilerParams(vmem_limit_bytes=VMEM_BYTES),
    )(q0, q1, q2, q3, precond, other)
    line = jnp.stack([piece] + [swap(piece, dz=k) for k in (1, 2, 3)])
    order, pieces = [], []
    for dy, dx in ((0, 0), (1, 1), (0, 1), (1, 0)):
        got = swap(line, dy=dy, dx=dx) if dy or dx else line
        order += [(dy, dx, 0), (dy, dx, 1)]
        pieces += [got, swap(got, dc=1)]
    rows = 128
    return pl.pallas_call(
        functools.partial(score_kernel, order),
        grid=(doc_count // rows,),
        out_shape=jax.ShapeDtypeStruct((doc_count, 128), F32),
        in_specs=[pl.BlockSpec((rows, width), lambda i: (i, 0))] + [vmem] * 8,
        out_specs=pl.BlockSpec((rows, 128), lambda i: (i, 0)),
        scratch_shapes=[pltpu.VMEM((128, width), BF16), pltpu.VMEM((128, width), BF16)],
        compiler_params=pltpu.CompilerParams(vmem_limit_bytes=VMEM_BYTES),
    )(documents, *pieces)


def general(documents, queries, precond):
    panels, _, panel_width = precond.shape
    width = documents.shape[1]
    asked = lax.all_gather(queries, "row", axis=0, tiled=True)
    asked = asked.reshape(asked.shape[0], panels, panel_width)
    own = jnp.einsum("qbk,brk->bqr", asked, precond, preferred_element_type=F32).astype(BF16)
    ready = lax.all_gather(own, "row", axis=0)
    ready = ready.transpose(2, 1, 0, 3).reshape(-1, width)
    raw = jnp.dot(documents, ready.T, preferred_element_type=F32)
    dense = documents.astype(F32)
    spread = jnp.sqrt(jnp.mean(dense * dense, axis=1) + 1e-06)
    return raw / (spread[:, None] * jnp.sqrt(F32(width)))


def solution(mesh):
    fits = mesh.shape["shard"] == 2 and mesh.shape["row"] == 16
    placed = (P(AXES, None), P("row", None), P(None, "row", None))
    return jax.shard_map(
        grouped if fits else general,
        mesh=mesh,
        in_specs=placed,
        out_specs=P(AXES, None),
        check_vma=False,
    )
```

```python
import jax
import jax.numpy as jnp
from jax import lax
from jax.experimental import pallas as pl
from jax.experimental.pallas import tpu as pltpu
from jax.sharding import PartitionSpec as P

AXES = ("shard", "row")
F32, BF16 = jnp.float32, jnp.bfloat16


def place():
    row = lax.axis_index("row")
    return lax.axis_index("shard"), row // 4, (row // 2) % 2, row % 2


def moved(array, source_of):
    pairs = []
    for index in range(32):
        here = (index // 16, index // 4 % 4, index // 2 % 2, index % 2)
        y, z, x, c = source_of(*here)
        pairs.append((y * 16 + z * 4 + x * 2 + c, index))
    return lax.ppermute(array, AXES, pairs)


def over_core(array):
    return moved(array, lambda y, z, x, c: (y, z, x, c ^ 1))


def condition_kernel(q0, q1, q2, q3, own, other, out, acc):
    _, z, _, c = place()
    panels, rows, width = own.shape
    for b in range(panels):
        at = slice(b * width, (b + 1) * width)
        asked = jnp.concatenate([q[:, at].astype(F32) for q in (q0, q1, q2, q3)], axis=0)
        block = jnp.concatenate([own[b], other[b]], axis=0)
        got = lax.dot_general(
            asked.astype(BF16), block, (((1,), (1,)), ((), ())), preferred_element_type=F32
        )
        got = pltpu.roll(got, c * rows, axis=1)
        for k in range(4):
            acc[pl.ds(pl.multiple_of((z ^ k) * 8, 8), 8), b * 128 : (b + 1) * 128] = got[
                k * 8 : (k + 1) * 8
            ]
    out[...] = acc[...].astype(BF16)


def norm_kernel(docs, own, after, kept, scale, own_kept, sems):
    count, width = docs.shape
    parts = 8
    rows = count // parts
    copies = [
        pltpu.make_async_copy(
            docs.at[pl.ds(i * rows, rows)], kept.at[pl.ds(i * rows, rows)], sems.at[i]
        )
        for i in range(parts)
    ]
    last = pltpu.make_async_copy(own, own_kept, sems.at[parts])
    for copy in copies:
        copy.start()
    last.start()
    for i, copy in enumerate(copies):
        copy.wait()
        total = jnp.zeros((rows, 128), F32)
        for at in range(0, width, 128):
            dense = kept[i * rows : (i + 1) * rows, at : at + 128].astype(F32)
            total += dense * dense
        mean = jnp.sum(total, axis=1, keepdims=True) * (1.0 / width)
        value = lax.rsqrt(mean + 1e-06) * (1.0 / width**0.5)
        scale[i * rows : (i + 1) * rows] = jnp.broadcast_to(value, (rows, 128))
    last.wait()


def assemble(pieces, held, ready, z):
    for slot, piece in pieces:
        rows = pl.ds(pl.multiple_of(slot * 32, 32), 32)
        for k in range(4):
            for b in range(4):
                start = b * 512 + (z ^ k) * 128
                held[rows, pl.ds(pl.multiple_of(start, 128), 128)] = piece[
                    k, :, b * 128 : (b + 1) * 128
                ]
    width = held.shape[1]
    step = 512
    for at in range(0, width, step):
        part = held[:, at : at + step].astype(F32).reshape(4, 4, 8, step)
        part = jnp.concatenate([part[s, k] for k in range(4) for s in range(4)], axis=0)
        ready[:, at : at + step] = part.astype(BF16)


def columns(docs, at, rows, side):
    parts = []
    for block in range(16):
        start = pl.multiple_of(block * 256 + side * 128, 128)
        parts.append(docs[pl.ds(at, rows), pl.ds(start, 128)])
    return jnp.concatenate(parts, axis=1)


def times(left, right):
    return lax.dot_general(left, right, (((1,), (1,)), ((), ())), preferred_element_type=F32)


def near_kernel(docs, line, line_c, first, second, first_c, second_c, out, held, ready):
    y, z, x, c = place()
    s = x ^ y

    def fill(own, across, own_c, across_c):
        assemble(
            [
                (s * 2 + c, own),
                ((1 - s) * 2 + c, across),
                (s * 2 + 1 - c, own_c),
                ((1 - s) * 2 + 1 - c, across_c),
            ],
            held,
            ready,
            z,
        )

    @pl.when(c == 0)
    def _():
        fill(line, second, line_c, first_c)

    @pl.when(c == 1)
    def _():
        fill(line, first, line_c, second_c)

    rows = 256
    for at in range(0, docs.shape[0], rows):
        out[at : at + rows] = times(columns(docs, at, rows, x), ready[...])


def far_kernel(
    docs, scale, near, third, first, second, third_c, first_c, second_c, out, held, ready, made, sems
):
    y, z, x, c = place()
    s = x ^ y

    def fill(diagonal, beside, diagonal_c, beside_c):
        assemble(
            [
                (s * 2 + c, diagonal),
                ((1 - s) * 2 + c, beside),
                (s * 2 + 1 - c, diagonal_c),
                ((1 - s) * 2 + 1 - c, beside_c),
            ],
            held,
            ready,
            z,
        )

    @pl.when(c == 0)
    def _():
        fill(third, first, third_c, second_c)

    @pl.when(c == 1)
    def _():
        fill(third, second, third_c, first_c)

    rows = 256
    copies = []
    for i, at in enumerate(range(0, docs.shape[0], rows)):
        got = times(columns(docs, at, rows, 1 - x), ready[...])
        made[at : at + rows] = (near[at : at + rows] + got) * scale[at : at + rows]
        copies.append(
            pltpu.make_async_copy(
                made.at[pl.ds(at, rows)], out.at[pl.ds(at, rows)], sems.at[i]
            )
        )
        copies[-1].start()
    for copy in copies:
        copy.wait()


def in_hbm(array):
    return pltpu.with_memory_space_constraint(array, pltpu.HBM)


def call(kernel, inputs, specs, outs, out_specs, scratch, flops, moved_bytes, limit):
    return pl.pallas_call(
        kernel,
        out_shape=outs,
        in_specs=specs,
        out_specs=out_specs,
        scratch_shapes=scratch,
        cost_estimate=pl.CostEstimate(flops=flops, bytes_accessed=moved_bytes, transcendentals=0),
        compiler_params=pltpu.CompilerParams(vmem_limit_bytes=limit),
    )(*inputs)


def grouped(documents, queries, precond):
    count, width = documents.shape
    vmem, anywhere = pl.BlockSpec(memory_space=pltpu.VMEM), pl.BlockSpec(memory_space=pltpu.HBM)
    like = jax.ShapeDtypeStruct
    mib = 1024 * 1024

    other = over_core(precond)
    asked = {}
    for k in (3, 2):
        asked[k] = moved(queries, lambda y, z, x, c: (y, z ^ k, x ^ y, c))
    queries, other = lax.optimization_barrier((queries, other))
    for k in (1, 0):
        asked[k] = moved(queries, lambda y, z, x, c: (y, z ^ k, x ^ y, c))
    kept, scale, own = call(
        norm_kernel,
        (in_hbm(documents), in_hbm(precond), other),
        [anywhere, anywhere, pl.BlockSpec(memory_space=pl.ANY)],
        (like((count, width), BF16), like((count, 128), F32), like(precond.shape, BF16)),
        (vmem,) * 3,
        [pltpu.SemaphoreType.DMA((9,))],
        count * width * 2,
        count * width * 2,
        2 * mib,
    )
    piece = call(
        condition_kernel,
        (*[asked[k] for k in range(4)], own, other),
        [vmem] * 6,
        like((32, 512), BF16),
        vmem,
        [pltpu.VMEM((32, 512), F32)],
        2 * 32 * 512 * 1024,
        mib,
        4 * mib,
    )
    line = jnp.stack([piece] + [moved(piece, lambda y, z, x, c: (y, z ^ k, x, c)) for k in (1, 2, 3)])
    first = moved(line, lambda y, z, x, c: (y ^ c, z, x ^ 1 ^ c, c))
    second = moved(line, lambda y, z, x, c: (y ^ 1 ^ c, z, x ^ c, c))
    third = moved(first, lambda y, z, x, c: (y ^ 1 ^ c, z, x ^ c, c))
    line_c, first_c, second_c, third_c = map(over_core, (line, first, second, third))
    half = [pltpu.VMEM((128, width // 2), BF16), pltpu.VMEM((128, width // 2), BF16)]
    near = call(
        near_kernel,
        (kept, line, line_c, first, second, first_c, second_c),
        [vmem] * 7,
        like((count, 128), F32),
        vmem,
        half,
        count * width * 128,
        count * width,
        12 * mib,
    )
    return call(
        far_kernel,
        (kept, scale, near, third, first, second, third_c, first_c, second_c),
        [vmem] * 9,
        like((count, 128), F32),
        anywhere,
        [*half, pltpu.VMEM((count, 128), F32), pltpu.SemaphoreType.DMA((4,))],
        count * width * 128,
        count * width,
        12 * mib,
    )


def general(documents, queries, precond):
    panels, _, panel_width = precond.shape
    width = documents.shape[1]
    asked = lax.all_gather(queries, "row", axis=0, tiled=True)
    asked = asked.reshape(asked.shape[0], panels, panel_width)
    own = jnp.einsum("qbk,brk->bqr", asked, precond, preferred_element_type=F32).astype(BF16)
    ready = lax.all_gather(own, "row", axis=0)
    ready = ready.transpose(2, 1, 0, 3).reshape(-1, width)
    raw = jnp.dot(documents, ready.T, preferred_element_type=F32)
    dense = documents.astype(F32)
    spread = jnp.sqrt(jnp.mean(dense * dense, axis=1) + 1e-06)
    return raw / (spread[:, None] * jnp.sqrt(F32(width)))


def solution(mesh):
    fits = mesh.shape["shard"] == 2 and mesh.shape["row"] == 16
    placed = (P(AXES, None), P("row", None), P(None, "row", None))
    return jax.shard_map(
        grouped if fits else general,
        mesh=mesh,
        in_specs=placed,
        out_specs=P(AXES, None),
        check_vma=False,
    )
```

```python
import jax
import jax.numpy as jnp
from jax import lax
from jax.experimental import pallas as pl
from jax.experimental.pallas import tpu as pltpu
from jax.sharding import PartitionSpec as P

AXES = ("shard", "row")
F32, BF16 = jnp.float32, jnp.bfloat16


def place():
    row = lax.axis_index("row")
    return lax.axis_index("shard"), row // 4, (row // 2) % 2, row % 2


def moved(array, source_of):
    pairs = []
    for index in range(32):
        here = (index // 16, index // 4 % 4, index // 2 % 2, index % 2)
        y, z, x, c = source_of(*here)
        pairs.append((y * 16 + z * 4 + x * 2 + c, index))
    return lax.ppermute(array, AXES, pairs)


def over_core(array):
    return moved(array, lambda y, z, x, c: (y, z, x, c ^ 1))


def parity(z):
    return z % 2


def spot(z):
    return parity(z) * 2 + z // 2


def condition_kernel(q0, q1, q2, q3, own, other, out, acc):
    _, z, _, c = place()
    panels, rows, width = own.shape
    for b in range(panels):
        at = slice(b * width, (b + 1) * width)
        asked = jnp.concatenate([q[:, at].astype(F32) for q in (q0, q1, q2, q3)], axis=0)
        block = jnp.concatenate([own[b], other[b]], axis=0)
        got = lax.dot_general(
            asked.astype(BF16), block, (((1,), (1,)), ((), ())), preferred_element_type=F32
        )
        got = pltpu.roll(got, c * rows, axis=1)
        for k in range(4):
            acc[pl.ds(pl.multiple_of(spot(z ^ k) * 8, 8), 8), b * 128 : (b + 1) * 128] = got[
                k * 8 : (k + 1) * 8
            ]
    out[...] = acc[...].astype(BF16)


def norm_kernel(docs, own, after, kept, scale, own_kept, sems):
    count, width = docs.shape
    parts = 8
    rows = count // parts
    copies = [
        pltpu.make_async_copy(
            docs.at[pl.ds(i * rows, rows)], kept.at[pl.ds(i * rows, rows)], sems.at[i]
        )
        for i in range(parts)
    ]
    last = pltpu.make_async_copy(own, own_kept, sems.at[parts])
    for copy in copies:
        copy.start()
    last.start()
    for i, copy in enumerate(copies):
        copy.wait()
        total = jnp.zeros((rows, 128), F32)
        for at in range(0, width, 128):
            dense = kept[i * rows : (i + 1) * rows, at : at + 128].astype(F32)
            total += dense * dense
        mean = jnp.sum(total, axis=1, keepdims=True) * (1.0 / width)
        value = lax.rsqrt(mean + 1e-06) * (1.0 / width**0.5)
        scale[i * rows : (i + 1) * rows] = jnp.broadcast_to(value, (rows, 128))
    last.wait()


def assemble(pieces, held, ready, z):
    for tilt, core, piece in pieces:
        for k in range(4):
            for group in range(2):
                side = tilt ^ parity(z ^ k) ^ group
                rows = pl.ds(pl.multiple_of((side * 2 + core) * 32 + group * 16, 16), 16)
                for b in range(4):
                    start = pl.multiple_of(b * 512 + (z ^ k) * 128, 128)
                    held[rows, pl.ds(start, 128)] = piece[
                        k, group * 16 : (group + 1) * 16, b * 128 : (b + 1) * 128
                    ]
    width = held.shape[1]
    step = 512
    for at in range(0, width, step):
        part = held[:, at : at + step].astype(F32).reshape(4, 4, 8, step)
        part = jnp.concatenate([part[s, spot(at_z)] for at_z in range(4) for s in range(4)], axis=0)
        ready[:, at : at + step] = part.astype(BF16)


def columns(docs, at, rows, side):
    parts = []
    for block in range(16):
        start = pl.multiple_of(block * 256 + side * 128, 128)
        parts.append(docs[pl.ds(at, rows), pl.ds(start, 128)])
    return jnp.concatenate(parts, axis=1)


def times(left, right):
    return lax.dot_general(left, right, (((1,), (1,)), ((), ())), preferred_element_type=F32)


def near_kernel(docs, own, own_c, across, across_c, out, held, ready):
    y, z, x, c = place()
    s = x ^ y
    assemble(
        ((s, c, own), (s, 1 - c, own_c), (1 - s, c, across), (1 - s, 1 - c, across_c)), held, ready, z
    )
    rows = 256
    for at in range(0, docs.shape[0], rows):
        out[at : at + rows] = times(columns(docs, at, rows, x), ready[...])


def far_kernel(
    docs, scale, near, diagonal, diagonal_c, beside, beside_c, out, held, ready, made, sems
):
    y, z, x, c = place()
    s = x ^ y
    assemble(
        ((s, c, diagonal), (s, 1 - c, diagonal_c), (1 - s, c, beside), (1 - s, 1 - c, beside_c)),
        held,
        ready,
        z,
    )
    rows = 256
    copies = []
    for i, at in enumerate(range(0, docs.shape[0], rows)):
        got = times(columns(docs, at, rows, 1 - x), ready[...])
        made[at : at + rows] = (near[at : at + rows] + got) * scale[at : at + rows]
        copies.append(
            pltpu.make_async_copy(
                made.at[pl.ds(at, rows)], out.at[pl.ds(at, rows)], sems.at[i]
            )
        )
        copies[-1].start()
    for copy in copies:
        copy.wait()


def in_hbm(array):
    return pltpu.with_memory_space_constraint(array, pltpu.HBM)


def call(kernel, inputs, specs, outs, out_specs, scratch, flops, moved_bytes, limit):
    return pl.pallas_call(
        kernel,
        out_shape=outs,
        in_specs=specs,
        out_specs=out_specs,
        scratch_shapes=scratch,
        cost_estimate=pl.CostEstimate(flops=flops, bytes_accessed=moved_bytes, transcendentals=0),
        compiler_params=pltpu.CompilerParams(vmem_limit_bytes=limit),
    )(*inputs)


def grouped(documents, queries, precond):
    count, width = documents.shape
    vmem, anywhere = pl.BlockSpec(memory_space=pltpu.VMEM), pl.BlockSpec(memory_space=pltpu.HBM)
    like = jax.ShapeDtypeStruct
    mib = 1024 * 1024

    other = over_core(precond)
    asked = {}
    for k in (3,2):
        asked[k] = moved(queries, lambda y, z, x, c: (y, z ^ k, x ^ y ^ parity(k), c))
    queries, other = lax.optimization_barrier((queries, other))
    for k in (1,0):
        asked[k] = moved(queries, lambda y, z, x, c: (y, z ^ k, x ^ y ^ parity(k), c))
    kept, scale, own = call(
        norm_kernel,
        (in_hbm(documents), in_hbm(precond), other),
        [anywhere, anywhere, pl.BlockSpec(memory_space=pl.ANY)],
        (like((count, width), BF16), like((count, 128), F32), like(precond.shape, BF16)),
        (vmem,) * 3,
        [pltpu.SemaphoreType.DMA((9,))],
        count * width * 2,
        count * width * 2,
        2 * mib,
    )
    piece = call(
        condition_kernel,
        (*[asked[k] for k in range(4)], own, other),
        [vmem] * 6,
        like((32, 512), BF16),
        vmem,
        [pltpu.VMEM((32, 512), F32)],
        2 * 32 * 512 * 1024,
        mib,
        4 * mib,
    )
    line = jnp.stack([piece] + [moved(piece, lambda y, z, x, c: (y, z ^ k, x, c)) for k in (1, 2, 3)])
    diagonal = moved(line, lambda y, z, x, c: (y ^ 1, z, x ^ 1, c))
    beside = moved(line, lambda y, z, x, c: (y, z, x ^ 1, c))
    across = moved(line, lambda y, z, x, c: (y ^ 1, z, x, c))
    line_c, across_c, beside_c, diagonal_c = map(over_core, (line, across, beside, diagonal))
    half = [pltpu.VMEM((128, width // 2), BF16), pltpu.VMEM((128, width // 2), BF16)]
    near = call(
        near_kernel,
        (kept, line, line_c, across, across_c),
        [vmem] * 5,
        like((count, 128), F32),
        vmem,
        half,
        count * width * 128,
        count * width,
        12 * mib,
    )
    return call(
        far_kernel,
        (kept, scale, near, diagonal, diagonal_c, beside, beside_c),
        [vmem] * 7,
        like((count, 128), F32),
        anywhere,
        [*half, pltpu.VMEM((count, 128), F32), pltpu.SemaphoreType.DMA((4,))],
        count * width * 128,
        count * width,
        12 * mib,
    )


def general(documents, queries, precond):
    panels, _, panel_width = precond.shape
    width = documents.shape[1]
    asked = lax.all_gather(queries, "row", axis=0, tiled=True)
    asked = asked.reshape(asked.shape[0], panels, panel_width)
    own = jnp.einsum("qbk,brk->bqr", asked, precond, preferred_element_type=F32).astype(BF16)
    ready = lax.all_gather(own, "row", axis=0)
    ready = ready.transpose(2, 1, 0, 3).reshape(-1, width)
    raw = jnp.dot(documents, ready.T, preferred_element_type=F32)
    dense = documents.astype(F32)
    spread = jnp.sqrt(jnp.mean(dense * dense, axis=1) + 1e-06)
    return raw / (spread[:, None] * jnp.sqrt(F32(width)))


def solution(mesh):
    fits = mesh.shape["shard"] == 2 and mesh.shape["row"] == 16
    placed = (P(AXES, None), P("row", None), P(None, "row", None))
    return jax.shard_map(
        grouped if fits else general,
        mesh=mesh,
        in_specs=placed,
        out_specs=P(AXES, None),
        check_vma=False,
    )
```

```python
import jax
import jax.numpy as jnp
from jax import lax
from jax.experimental import pallas as pl
from jax.experimental.pallas import tpu as pltpu
from jax.sharding import PartitionSpec as P

AXES = ("shard", "row")
F32, BF16 = jnp.float32, jnp.bfloat16


def place():
    row = lax.axis_index("row")
    return lax.axis_index("shard"), row // 4, (row // 2) % 2, row % 2


def moved(array, source_of):
    pairs = []
    for index in range(32):
        here = (index // 16, index // 4 % 4, index // 2 % 2, index % 2)
        y, z, x, c = source_of(*here)
        pairs.append((y * 16 + z * 4 + x * 2 + c, index))
    return lax.ppermute(array, AXES, pairs)


def over_core(array):
    return moved(array, lambda y, z, x, c: (y, z, x, c ^ 1))


def asked_of(turn, y, c):
    dz = turn * 3 ^ c * 1
    return dz, y ^ dz % 2


def condition_kernel(asked0, asked1, own, other, out):
    c = place()[3]
    panels, rows, width = own.shape
    for b in range(panels):
        at = slice(b * width, (b + 1) * width)
        asked = jnp.concatenate([asked0[:, at], asked1[:, at]], axis=0)
        block = jnp.concatenate([own[b], other[b]], axis=0)
        got = pltpu.roll(times(asked, block), c * rows, axis=1)
        first = [got[turn * 16 : turn * 16 + 8] for turn in range(2)]
        second = [got[turn * 16 + 8 : turn * 16 + 16] for turn in range(2)]
        mine = [jnp.where(c == 0, f, s) for f, s in zip(first, second, strict=True)]
        theirs = [jnp.where(c == 0, s, f) for f, s in zip(first, second, strict=True)]
        out[:, b * 128 : (b + 1) * 128] = jnp.concatenate(
            [mine[0], theirs[0], mine[1], theirs[1]], axis=0
        ).astype(BF16)


def take(docs, first, kept, scale, sems):
    count, width = kept.shape
    parts = 4
    rows = count // parts
    copies = [
        pltpu.make_async_copy(
            docs.at[pl.ds(first + i * rows, rows)], kept.at[pl.ds(i * rows, rows)], sems.at[i]
        )
        for i in range(parts)
    ]
    for copy in copies:
        copy.start()
    for i, copy in enumerate(copies):
        copy.wait()
        total = jnp.zeros((rows, 128), F32)
        for at in range(0, width, 128):
            dense = kept[i * rows : (i + 1) * rows, at : at + 128].astype(F32)
            total += dense * dense
        mean = jnp.sum(total, axis=1, keepdims=True) * (1.0 / width)
        value = lax.rsqrt(mean + 1e-06) * (1.0 / width**0.5)
        scale[i * rows : (i + 1) * rows] = jnp.broadcast_to(value, (rows, 128))


def upper_kernel(docs, own, after, kept, scale, own_kept, sems):
    last = pltpu.make_async_copy(own, own_kept, sems.at[4])
    last.start()
    take(docs, 0, kept, scale, sems)
    last.wait()


def lower_kernel(docs, after, kept, scale, sems):
    take(docs, kept.shape[0], kept, scale, sems)


def assemble(pieces, ready, z):
    for x, y, core, piece in pieces:
        for k in range(4):
            for turn in range(2):
                dz, dx = asked_of(turn, y, core)
                start = (z ^ k ^ dz) * 32 + (x ^ dx) * 16
                rows = pl.ds(pl.multiple_of(start, 16), 16)
                for b in range(4):
                    start = pl.multiple_of(b * 512 + (z ^ k) * 128, 128)
                    ready[rows, pl.ds(start, 128)] = piece[
                        k, turn * 16 : (turn + 1) * 16, b * 128 : (b + 1) * 128
                    ]


def columns(docs, at, rows, side):
    parts = []
    for block in range(16):
        start = pl.multiple_of(block * 256 + side * 128, 128)
        parts.append(docs[pl.ds(at, rows), pl.ds(start, 128)])
    return jnp.concatenate(parts, axis=1)


def times(left, right):
    return lax.dot_general(left, right, (((1,), (1,)), ((), ())), preferred_element_type=F32)


def near_kernel(upper, lower, own, own_c, across, across_c, out, ready):
    y, z, x, c = place()
    assemble(
        ((x, y, c, own), (x, y, 1 - c, own_c), (x, 1 - y, c, across), (x, 1 - y, 1 - c, across_c)),
        ready,
        z,
    )
    count, rows = upper.shape[0], 256
    for half, docs in enumerate((upper, lower)):
        for at in range(0, count, rows):
            out[half * count + at : half * count + at + rows] = times(
                columns(docs, at, rows, x), ready[...]
            )


def far_kernel(
    upper,
    lower,
    upper_scale,
    lower_scale,
    near,
    diagonal,
    diagonal_c,
    beside,
    beside_c,
    out,
    ready,
    made,
    sems,
):
    y, z, x, c = place()
    assemble(
        (
            (1 - x, 1 - y, c, diagonal),
            (1 - x, 1 - y, 1 - c, diagonal_c),
            (1 - x, y, c, beside),
            (1 - x, y, 1 - c, beside_c),
        ),
        ready,
        z,
    )
    count, rows = upper.shape[0], 256
    copies = []
    for half, (docs, scale) in enumerate(((upper, upper_scale), (lower, lower_scale))):
        for at in range(0, count, rows):
            here = half * count + at
            got = times(columns(docs, at, rows, 1 - x), ready[...])
            made[here : here + rows] = (near[here : here + rows] + got) * scale[at : at + rows]
            copies.append(
                pltpu.make_async_copy(
                    made.at[pl.ds(here, rows)], out.at[pl.ds(here, rows)], sems.at[len(copies)]
                )
            )
            copies[-1].start()
    for copy in copies:
        copy.wait()


def in_hbm(array):
    return pltpu.with_memory_space_constraint(array, pltpu.HBM)


def call(kernel, inputs, specs, outs, out_specs, scratch, flops, moved_bytes, limit):
    return pl.pallas_call(
        kernel,
        out_shape=outs,
        in_specs=specs,
        out_specs=out_specs,
        scratch_shapes=scratch,
        cost_estimate=pl.CostEstimate(flops=flops, bytes_accessed=moved_bytes, transcendentals=0),
        compiler_params=pltpu.CompilerParams(vmem_limit_bytes=limit),
    )(*inputs)


def grouped(documents, queries, precond):
    count, width = documents.shape
    vmem, anywhere = pl.BlockSpec(memory_space=pltpu.VMEM), pl.BlockSpec(memory_space=pltpu.HBM)
    like = jax.ShapeDtypeStruct
    mib = 1024 * 1024

    paired = over_core(queries)
    both = jnp.concatenate([queries, paired], axis=0)
    other = over_core(precond)

    def turned(turn):
        def source(y, z, x, c):
            dz, dx = asked_of(turn, y, c)
            return y, z ^ dz, x ^ dx, c

        return moved(both, source)

    asked = {turn: turned(turn) for turn in (1, 0)}
    half_docs, lanes = like((count // 2, width), BF16), like((count // 2, 128), F32)
    upper, upper_scale, own = call(
        upper_kernel,
        (in_hbm(documents), in_hbm(precond), other),
        [anywhere, anywhere, pl.BlockSpec(memory_space=pl.ANY)],
        (half_docs, lanes, like(precond.shape, BF16)),
        (vmem,) * 3,
        [pltpu.SemaphoreType.DMA((5,))],
        count * width,
        count * width,
        2 * mib,
    )
    piece = call(
        condition_kernel,
        (asked[0], asked[1], own, other),
        [vmem] * 4,
        like((32, 512), BF16),
        vmem,
        [],
        2 * 32 * 512 * 1024,
        mib,
        4 * mib,
    )
    line = jnp.stack([piece] + [moved(piece, lambda y, z, x, c: (y, z ^ k, x, c)) for k in (1, 2, 3)])
    diagonal = moved(line, lambda y, z, x, c: (y ^ 1, z, x ^ 1, c))
    beside = moved(line, lambda y, z, x, c: (y, z, x ^ 1, c))
    across = moved(line, lambda y, z, x, c: (y ^ 1, z, x, c))
    lower, lower_scale = call(
        lower_kernel,
        (in_hbm(documents), line),
        [anywhere, pl.BlockSpec(memory_space=pl.ANY)],
        (half_docs, lanes),
        (vmem,) * 2,
        [pltpu.SemaphoreType.DMA((4,))],
        count * width,
        count * width,
        2 * mib,
    )
    across, lower_scale = lax.optimization_barrier((across, lower_scale))
    line_c, across_c, beside_c, diagonal_c = map(over_core, (line, across, beside, diagonal))
    half = [pltpu.VMEM((128, width // 2), BF16)]
    near = call(
        near_kernel,
        (upper, lower, line, line_c, across, across_c),
        [vmem] * 6,
        like((count, 128), F32),
        vmem,
        half,
        count * width * 128,
        count * width,
        12 * mib,
    )
    return call(
        far_kernel,
        (upper, lower, upper_scale, lower_scale, near, diagonal, diagonal_c, beside, beside_c),
        [vmem] * 9,
        like((count, 128), F32),
        anywhere,
        [*half, pltpu.VMEM((count, 128), F32), pltpu.SemaphoreType.DMA((4,))],
        count * width * 128,
        count * width,
        12 * mib,
    )


def general(documents, queries, precond):
    panels, _, panel_width = precond.shape
    width = documents.shape[1]
    asked = lax.all_gather(queries, "row", axis=0, tiled=True)
    asked = asked.reshape(asked.shape[0], panels, panel_width)
    own = jnp.einsum("qbk,brk->bqr", asked, precond, preferred_element_type=F32).astype(BF16)
    ready = lax.all_gather(own, "row", axis=0)
    ready = ready.transpose(2, 1, 0, 3).reshape(-1, width)
    raw = jnp.dot(documents, ready.T, preferred_element_type=F32)
    dense = documents.astype(F32)
    spread = jnp.sqrt(jnp.mean(dense * dense, axis=1) + 1e-06)
    return raw / (spread[:, None] * jnp.sqrt(F32(width)))


def solution(mesh):
    fits = mesh.shape["shard"] == 2 and mesh.shape["row"] == 16
    placed = (P(AXES, None), P("row", None), P(None, "row", None))
    return jax.shard_map(
        grouped if fits else general,
        mesh=mesh,
        in_specs=placed,
        out_specs=P(AXES, None),
        check_vma=False,
    )
```

```python
import jax
import jax.numpy as jnp
from jax import lax
from jax.experimental import pallas as pl
from jax.experimental.pallas import tpu as pltpu
from jax.sharding import PartitionSpec as P

AXES = ("shard", "row")
F32, BF16 = jnp.float32, jnp.bfloat16


def place():
    row = lax.axis_index("row")
    return lax.axis_index("shard"), row // 4, (row // 2) % 2, row % 2


def moved(array, source_of):
    pairs = []
    for index in range(32):
        here = (index // 16, index // 4 % 4, index // 2 % 2, index % 2)
        y, z, x, c = source_of(*here)
        pairs.append((y * 16 + z * 4 + x * 2 + c, index))
    return lax.ppermute(array, AXES, pairs)


def over_core(array):
    return moved(array, lambda y, z, x, c: (y, z, x, c ^ 1))


def asked_of(turn, y, c):
    dz = turn * 3 ^ c * 1
    return dz, y ^ dz % 2


def condition_kernel(asked0, asked1, own, other, out):
    c = place()[3]
    panels, rows, width = own.shape
    for b in range(panels):
        at = slice(b * width, (b + 1) * width)
        asked = jnp.concatenate([asked0[:, at], asked1[:, at]], axis=0)
        block = jnp.concatenate([own[b], other[b]], axis=0)
        got = pltpu.roll(times(asked, block), c * rows, axis=1)
        first = [got[turn * 16 : turn * 16 + 8] for turn in range(2)]
        second = [got[turn * 16 + 8 : turn * 16 + 16] for turn in range(2)]
        mine = [jnp.where(c == 0, f, s) for f, s in zip(first, second, strict=True)]
        theirs = [jnp.where(c == 0, s, f) for f, s in zip(first, second, strict=True)]
        out[:, b * 128 : (b + 1) * 128] = jnp.concatenate(
            [mine[0], theirs[0], mine[1], theirs[1]], axis=0
        ).astype(BF16)


def take(docs, first, kept, scale, sems):
    count, width = kept.shape
    parts = 4
    rows = count // parts
    copies = [
        pltpu.make_async_copy(
            docs.at[pl.ds(first + i * rows, rows)], kept.at[pl.ds(i * rows, rows)], sems.at[i]
        )
        for i in range(parts)
    ]
    for copy in copies:
        copy.start()
    for i, copy in enumerate(copies):
        copy.wait()
        total = jnp.zeros((rows, 128), F32)
        for at in range(0, width, 128):
            dense = kept[i * rows : (i + 1) * rows, at : at + 128].astype(F32)
            total += dense * dense
        mean = jnp.sum(total, axis=1, keepdims=True) * (1.0 / width)
        value = lax.rsqrt(mean + 1e-06) * (1.0 / width**0.5)
        scale[i * rows : (i + 1) * rows] = jnp.broadcast_to(value, (rows, 128))


def upper_kernel(docs, own, after, kept, scale, own_kept, sems):
    last = pltpu.make_async_copy(own, own_kept, sems.at[4])
    last.start()
    take(docs, 0, kept, scale, sems)
    last.wait()


def lower_kernel(docs, after, kept, scale, sems):
    take(docs, kept.shape[0], kept, scale, sems)


def assemble(pieces, ready, z):
    for b, panel in enumerate(ready):
        for x, y, core, piece in pieces:
            for k in range(4):
                for turn in range(2):
                    dz, dx = asked_of(turn, y, core)
                    start = (z ^ k ^ dz) * 32 + (x ^ dx) * 16
                    rows = pl.ds(pl.multiple_of(start, 16), 16)
                    start = pl.multiple_of((z ^ k) * 128, 128)
                    panel[rows, pl.ds(start, 128)] = piece[
                        k, turn * 16 : (turn + 1) * 16, b * 128 : (b + 1) * 128
                    ]


def columns(docs, at, rows, side, b):
    parts = []
    for block in range(b * 4, b * 4 + 4):
        start = pl.multiple_of(block * 256 + side * 128, 128)
        parts.append(docs[pl.ds(at, rows), pl.ds(start, 128)])
    return jnp.concatenate(parts, axis=1)


def product(docs, at, rows, side, ready):
    total = times(columns(docs, at, rows, side, 0), ready[0][...])
    for b in range(1, len(ready)):
        total += times(columns(docs, at, rows, side, b), ready[b][...])
    return total


def times(left, right):
    return lax.dot_general(left, right, (((1,), (1,)), ((), ())), preferred_element_type=F32)


def near_kernel(upper, lower, own, own_c, across, across_c, out, *ready):
    y, z, x, c = place()
    assemble(
        ((x, y, c, own), (x, y, 1 - c, own_c), (x, 1 - y, c, across), (x, 1 - y, 1 - c, across_c)),
        ready,
        z,
    )
    count, rows = upper.shape[0], 256
    for half, docs in enumerate((upper, lower)):
        for at in range(0, count, rows):
            out[half * count + at : half * count + at + rows] = product(docs, at, rows, x, ready)


def far_kernel(
    upper,
    lower,
    upper_scale,
    lower_scale,
    near,
    diagonal,
    diagonal_c,
    beside,
    beside_c,
    out,
    made,
    sems,
    *ready,
):
    y, z, x, c = place()
    assemble(
        (
            (1 - x, 1 - y, c, diagonal),
            (1 - x, 1 - y, 1 - c, diagonal_c),
            (1 - x, y, c, beside),
            (1 - x, y, 1 - c, beside_c),
        ),
        ready,
        z,
    )
    count, rows = upper.shape[0], 256
    copies = []
    for half, (docs, scale) in enumerate(((upper, upper_scale), (lower, lower_scale))):
        for at in range(0, count, rows):
            here = half * count + at
            got = product(docs, at, rows, 1 - x, ready)
            made[here : here + rows] = (near[here : here + rows] + got) * scale[at : at + rows]
            copies.append(
                pltpu.make_async_copy(
                    made.at[pl.ds(here, rows)], out.at[pl.ds(here, rows)], sems.at[len(copies)]
                )
            )
            copies[-1].start()
    for copy in copies:
        copy.wait()


def in_hbm(array):
    return pltpu.with_memory_space_constraint(array, pltpu.HBM)


def call(kernel, inputs, specs, outs, out_specs, scratch, flops, moved_bytes, limit):
    return pl.pallas_call(
        kernel,
        out_shape=outs,
        in_specs=specs,
        out_specs=out_specs,
        scratch_shapes=scratch,
        cost_estimate=pl.CostEstimate(flops=flops, bytes_accessed=moved_bytes, transcendentals=0),
        compiler_params=pltpu.CompilerParams(vmem_limit_bytes=limit),
    )(*inputs)


def grouped(documents, queries, precond):
    count, width = documents.shape
    vmem, anywhere = pl.BlockSpec(memory_space=pltpu.VMEM), pl.BlockSpec(memory_space=pltpu.HBM)
    like = jax.ShapeDtypeStruct
    mib = 1024 * 1024

    paired = over_core(queries)
    both = jnp.concatenate([queries, paired], axis=0)
    other = over_core(precond)

    def turned(turn):
        def source(y, z, x, c):
            dz, dx = asked_of(turn, y, c)
            return y, z ^ dz, x ^ dx, c

        return moved(both, source)

    asked = {turn: turned(turn) for turn in (1, 0)}
    half_docs, lanes = like((count // 2, width), BF16), like((count // 2, 128), F32)
    upper, upper_scale, own = call(
        upper_kernel,
        (in_hbm(documents), in_hbm(precond), other),
        [anywhere, anywhere, pl.BlockSpec(memory_space=pl.ANY)],
        (half_docs, lanes, like(precond.shape, BF16)),
        (vmem,) * 3,
        [pltpu.SemaphoreType.DMA((5,))],
        count * width,
        count * width,
        2 * mib,
    )
    piece = call(
        condition_kernel,
        (asked[0], asked[1], own, other),
        [vmem] * 4,
        like((32, 512), BF16),
        vmem,
        [],
        2 * 32 * 512 * 1024,
        mib,
        4 * mib,
    )
    line = jnp.stack([piece] + [moved(piece, lambda y, z, x, c: (y, z ^ k, x, c)) for k in (1, 2, 3)])
    diagonal = moved(line, lambda y, z, x, c: (y ^ 1, z, x ^ 1, c))
    beside = moved(line, lambda y, z, x, c: (y, z, x ^ 1, c))
    across = moved(line, lambda y, z, x, c: (y ^ 1, z, x, c))
    lower, lower_scale = call(
        lower_kernel,
        (in_hbm(documents), line),
        [anywhere, pl.BlockSpec(memory_space=pl.ANY)],
        (half_docs, lanes),
        (vmem,) * 2,
        [pltpu.SemaphoreType.DMA((4,))],
        count * width,
        count * width,
        2 * mib,
    )
    across, lower_scale = lax.optimization_barrier((across, lower_scale))
    line_c, across_c, beside_c, diagonal_c = map(over_core, (line, across, beside, diagonal))
    half = [pltpu.VMEM((128, width // 8), BF16)] * 4
    near = call(
        near_kernel,
        (upper, lower, line, line_c, across, across_c),
        [vmem] * 6,
        like((count, 128), F32),
        vmem,
        half,
        count * width * 128,
        count * width,
        12 * mib,
    )
    return call(
        far_kernel,
        (upper, lower, upper_scale, lower_scale, near, diagonal, diagonal_c, beside, beside_c),
        [vmem] * 9,
        like((count, 128), F32),
        anywhere,
        [pltpu.VMEM((count, 128), F32), pltpu.SemaphoreType.DMA((8,)), *half],
        count * width * 128,
        count * width,
        12 * mib,
    )


def general(documents, queries, precond):
    panels, _, panel_width = precond.shape
    width = documents.shape[1]
    asked = lax.all_gather(queries, "row", axis=0, tiled=True)
    asked = asked.reshape(asked.shape[0], panels, panel_width)
    own = jnp.einsum("qbk,brk->bqr", asked, precond, preferred_element_type=F32).astype(BF16)
    ready = lax.all_gather(own, "row", axis=0)
    ready = ready.transpose(2, 1, 0, 3).reshape(-1, width)
    raw = jnp.dot(documents, ready.T, preferred_element_type=F32)
    dense = documents.astype(F32)
    spread = jnp.sqrt(jnp.mean(dense * dense, axis=1) + 1e-06)
    return raw / (spread[:, None] * jnp.sqrt(F32(width)))


def solution(mesh):
    fits = mesh.shape["shard"] == 2 and mesh.shape["row"] == 16
    placed = (P(AXES, None), P("row", None), P(None, "row", None))
    return jax.shard_map(
        grouped if fits else general,
        mesh=mesh,
        in_specs=placed,
        out_specs=P(AXES, None),
        check_vma=False,
    )
```

```python
import jax
import jax.numpy as jnp
from jax import lax
from jax.experimental import pallas as pl
from jax.experimental.pallas import tpu as pltpu
from jax.sharding import PartitionSpec as P

AXES = ("shard", "row")
F32, BF16 = jnp.float32, jnp.bfloat16


def place():
    row = lax.axis_index("row")
    return lax.axis_index("shard"), row // 4, (row // 2) % 2, row % 2


def moved(array, source_of):
    pairs = []
    for index in range(32):
        here = (index // 16, index // 4 % 4, index // 2 % 2, index % 2)
        y, z, x, c = source_of(*here)
        pairs.append((y * 16 + z * 4 + x * 2 + c, index))
    return lax.ppermute(array, AXES, pairs)


def over_core(array):
    return moved(array, lambda y, z, x, c: (y, z, x, c ^ 1))


def asked_of(turn, y, c):
    dz = turn * 3 ^ c * 1
    return dz, y ^ dz % 2


def condition_kernel(asked0, asked1, own, other, out):
    c = place()[3]
    panels, rows, width = own.shape
    for b in range(panels):
        at = slice(b * width, (b + 1) * width)
        asked = jnp.concatenate([asked0[:, at], asked1[:, at]], axis=0)
        block = jnp.concatenate([own[b], other[b]], axis=0)
        got = pltpu.roll(times(asked, block), c * rows, axis=1)
        first = [got[turn * 16 : turn * 16 + 8] for turn in range(2)]
        second = [got[turn * 16 + 8 : turn * 16 + 16] for turn in range(2)]
        mine = [jnp.where(c == 0, f, s) for f, s in zip(first, second, strict=True)]
        theirs = [jnp.where(c == 0, s, f) for f, s in zip(first, second, strict=True)]
        out[:, b * 128 : (b + 1) * 128] = jnp.concatenate(
            [mine[0], theirs[0], mine[1], theirs[1]], axis=0
        ).astype(BF16)


def take(docs, first, kept, scale, sems):
    count, width = kept.shape
    parts = 4
    rows = count // parts
    copies = [
        pltpu.make_async_copy(
            docs.at[pl.ds(first + i * rows, rows)], kept.at[pl.ds(i * rows, rows)], sems.at[i]
        )
        for i in range(parts)
    ]
    for copy in copies:
        copy.start()
    for i, copy in enumerate(copies):
        copy.wait()
        total = jnp.zeros((rows, 128), F32)
        for at in range(0, width, 128):
            dense = kept[i * rows : (i + 1) * rows, at : at + 128].astype(F32)
            total += dense * dense
        mean = jnp.sum(total, axis=1, keepdims=True) * (1.0 / width)
        value = lax.rsqrt(mean + 1e-06) * (1.0 / width**0.5)
        scale[i * rows : (i + 1) * rows] = jnp.broadcast_to(value, (rows, 128))


def upper_kernel(docs, own, after, kept, scale, own_kept, sems):
    last = pltpu.make_async_copy(own, own_kept, sems.at[4])
    last.start()
    take(docs, 0, kept, scale, sems)
    last.wait()


def lower_kernel(docs, after, kept, scale, sems):
    take(docs, kept.shape[0], kept, scale, sems)


def assemble(pieces, ready, z):
    for b, panel in enumerate(ready):
        for x, y, core, piece in pieces:
            for k in range(4):
                for turn in range(2):
                    dz, dx = asked_of(turn, y, core)
                    start = (z ^ k ^ dz) * 32 + (x ^ dx) * 16
                    rows = pl.ds(pl.multiple_of(start, 16), 16)
                    start = pl.multiple_of((z ^ k) * 128, 128)
                    panel[rows, pl.ds(start, 128)] = piece[
                        k, turn * 16 : (turn + 1) * 16, b * 128 : (b + 1) * 128
                    ]


def columns(docs, at, rows, side, b):
    parts = []
    for block in range(b * 4, b * 4 + 4):
        start = pl.multiple_of(block * 256 + side * 128, 128)
        parts.append(docs[pl.ds(at, rows), pl.ds(start, 128)])
    return jnp.concatenate(parts, axis=1)


def product(docs, at, rows, side, ready):
    total = times(columns(docs, at, rows, side, 0), ready[0][...])
    for b in range(1, len(ready)):
        total += times(columns(docs, at, rows, side, b), ready[b][...])
    return total


def times(left, right):
    return lax.dot_general(left, right, (((1,), (1,)), ((), ())), preferred_element_type=F32)


def near_kernel(upper, lower, own, own_c, across, across_c, out, *ready):
    y, z, x, c = place()
    assemble(
        ((x, y, c, own), (x, y, 1 - c, own_c), (x, 1 - y, c, across), (x, 1 - y, 1 - c, across_c)),
        ready,
        z,
    )
    count, rows = upper.shape[0], 256
    for half, docs in enumerate((upper, lower)):
        for at in range(0, count, rows):
            out[half * count + at : half * count + at + rows] = product(docs, at, rows, x, ready)


def far_kernel(
    upper,
    lower,
    upper_scale,
    lower_scale,
    near,
    diagonal,
    diagonal_c,
    beside,
    beside_c,
    out,
    made,
    sems,
    *ready,
):
    y, z, x, c = place()
    assemble(
        (
            (1 - x, 1 - y, c, diagonal),
            (1 - x, 1 - y, 1 - c, diagonal_c),
            (1 - x, y, c, beside),
            (1 - x, y, 1 - c, beside_c),
        ),
        ready,
        z,
    )
    count = upper.shape[0]
    copies = []
    for half, (docs, scale) in enumerate(((upper, upper_scale), (lower, lower_scale))):
        cuts = (0, 2, 4) if half == 0 else (0, 2, 3, 4)
        for low, high in zip(cuts, cuts[1:]):
            at, rows = low * count // 4, (high - low) * count // 4
            here = half * count + at
            got = product(docs, at, rows, 1 - x, ready)
            made[here : here + rows] = (near[here : here + rows] + got) * scale[at : at + rows]
            copies.append(
                pltpu.make_async_copy(
                    made.at[pl.ds(here, rows)], out.at[pl.ds(here, rows)], sems.at[len(copies)]
                )
            )
            copies[-1].start()
    for copy in copies:
        copy.wait()


def in_hbm(array):
    return pltpu.with_memory_space_constraint(array, pltpu.HBM)


def call(kernel, inputs, specs, outs, out_specs, scratch, flops, moved_bytes, limit):
    return pl.pallas_call(
        kernel,
        out_shape=outs,
        in_specs=specs,
        out_specs=out_specs,
        scratch_shapes=scratch,
        cost_estimate=pl.CostEstimate(flops=flops, bytes_accessed=moved_bytes, transcendentals=0),
        compiler_params=pltpu.CompilerParams(vmem_limit_bytes=limit),
    )(*inputs)


def grouped(documents, queries, precond):
    count, width = documents.shape
    vmem, anywhere = pl.BlockSpec(memory_space=pltpu.VMEM), pl.BlockSpec(memory_space=pltpu.HBM)
    like = jax.ShapeDtypeStruct
    mib = 1024 * 1024

    paired = over_core(queries)
    both = jnp.concatenate([queries, paired], axis=0)
    other = over_core(precond)

    def turned(turn):
        def source(y, z, x, c):
            dz, dx = asked_of(turn, y, c)
            return y, z ^ dz, x ^ dx, c

        return moved(both, source)

    asked = {turn: turned(turn) for turn in (1, 0)}
    half_docs, lanes = like((count // 2, width), BF16), like((count // 2, 128), F32)
    upper, upper_scale, own = call(
        upper_kernel,
        (in_hbm(documents), in_hbm(precond), other),
        [anywhere, anywhere, pl.BlockSpec(memory_space=pl.ANY)],
        (half_docs, lanes, like(precond.shape, BF16)),
        (vmem,) * 3,
        [pltpu.SemaphoreType.DMA((5,))],
        count * width,
        count * width,
        2 * mib,
    )
    piece = call(
        condition_kernel,
        (asked[0], asked[1], own, other),
        [vmem] * 4,
        like((32, 512), BF16),
        vmem,
        [],
        2 * 32 * 512 * 1024,
        mib,
        4 * mib,
    )
    line = jnp.stack([piece] + [moved(piece, lambda y, z, x, c: (y, z ^ k, x, c)) for k in (1, 2, 3)])
    diagonal = moved(line, lambda y, z, x, c: (y ^ 1, z, x ^ 1, c))
    beside = moved(line, lambda y, z, x, c: (y, z, x ^ 1, c))
    across = moved(line, lambda y, z, x, c: (y ^ 1, z, x, c))
    lower, lower_scale = call(
        lower_kernel,
        (in_hbm(documents), line),
        [anywhere, pl.BlockSpec(memory_space=pl.ANY)],
        (half_docs, lanes),
        (vmem,) * 2,
        [pltpu.SemaphoreType.DMA((4,))],
        count * width,
        count * width,
        2 * mib,
    )
    across, lower_scale = lax.optimization_barrier((across, lower_scale))
    line_c, across_c, beside_c, diagonal_c = map(over_core, (line, across, beside, diagonal))
    half = [pltpu.VMEM((128, width // 8), BF16)] * 4
    near = call(
        near_kernel,
        (upper, lower, line, line_c, across, across_c),
        [vmem] * 6,
        like((count, 128), F32),
        vmem,
        half,
        count * width * 128,
        count * width,
        12 * mib,
    )
    return call(
        far_kernel,
        (upper, lower, upper_scale, lower_scale, near, diagonal, diagonal_c, beside, beside_c),
        [vmem] * 9,
        like((count, 128), F32),
        anywhere,
        [pltpu.VMEM((count, 128), F32), pltpu.SemaphoreType.DMA((8,)), *half],
        count * width * 128,
        count * width,
        12 * mib,
    )


def general(documents, queries, precond):
    panels, _, panel_width = precond.shape
    width = documents.shape[1]
    asked = lax.all_gather(queries, "row", axis=0, tiled=True)
    asked = asked.reshape(asked.shape[0], panels, panel_width)
    own = jnp.einsum("qbk,brk->bqr", asked, precond, preferred_element_type=F32).astype(BF16)
    ready = lax.all_gather(own, "row", axis=0)
    ready = ready.transpose(2, 1, 0, 3).reshape(-1, width)
    raw = jnp.dot(documents, ready.T, preferred_element_type=F32)
    dense = documents.astype(F32)
    spread = jnp.sqrt(jnp.mean(dense * dense, axis=1) + 1e-06)
    return raw / (spread[:, None] * jnp.sqrt(F32(width)))


def solution(mesh):
    fits = mesh.shape["shard"] == 2 and mesh.shape["row"] == 16
    placed = (P(AXES, None), P("row", None), P(None, "row", None))
    return jax.shard_map(
        grouped if fits else general,
        mesh=mesh,
        in_specs=placed,
        out_specs=P(AXES, None),
        check_vma=False,
    )
```

```python
import jax
import jax.numpy as jnp
from jax import lax
from jax.experimental import pallas as pl
from jax.experimental.pallas import tpu as pltpu
from jax.sharding import PartitionSpec as P

AXES = ("shard", "row")
F32, BF16 = jnp.float32, jnp.bfloat16


def place():
    row = lax.axis_index("row")
    return lax.axis_index("shard"), row // 4, (row // 2) % 2, row % 2


def moved(array, source_of):
    pairs = []
    for index in range(32):
        here = (index // 16, index // 4 % 4, index // 2 % 2, index % 2)
        y, z, x, c = source_of(*here)
        pairs.append((y * 16 + z * 4 + x * 2 + c, index))
    return lax.ppermute(array, AXES, pairs)


def over_core(array):
    return moved(array, lambda y, z, x, c: (y, z, x, c ^ 1))


def asked_of(turn, y, c):
    dz = turn * 3 ^ c * 1
    return dz, y ^ dz % 2


def condition_kernel(asked0, asked1, own, other, out):
    c = place()[3]
    panels, rows, width = own.shape
    for b in range(panels):
        at = slice(b * width, (b + 1) * width)
        asked = jnp.concatenate([asked0[:, at], asked1[:, at]], axis=0)
        block = jnp.concatenate([own[b], other[b]], axis=0)
        got = pltpu.roll(times(asked, block), c * rows, axis=1)
        first = [got[turn * 16 : turn * 16 + 8] for turn in range(2)]
        second = [got[turn * 16 + 8 : turn * 16 + 16] for turn in range(2)]
        mine = [jnp.where(c == 0, f, s) for f, s in zip(first, second, strict=True)]
        theirs = [jnp.where(c == 0, s, f) for f, s in zip(first, second, strict=True)]
        out[:, b * 128 : (b + 1) * 128] = jnp.concatenate(
            [mine[0], theirs[0], mine[1], theirs[1]], axis=0
        ).astype(BF16)


def take(docs, first, kept, scale, sems):
    count, width = kept.shape
    parts = 4
    rows = count // parts
    copies = [
        pltpu.make_async_copy(
            docs.at[pl.ds(first + i * rows, rows)], kept.at[pl.ds(i * rows, rows)], sems.at[i]
        )
        for i in range(parts)
    ]
    for copy in copies:
        copy.start()
    for i, copy in enumerate(copies):
        copy.wait()
        total = jnp.zeros((rows, 128), F32)
        for at in range(0, width, 128):
            dense = kept[i * rows : (i + 1) * rows, at : at + 128].astype(F32)
            total += dense * dense
        mean = jnp.sum(total, axis=1, keepdims=True) * (1.0 / width)
        value = lax.rsqrt(mean + 1e-06) * (1.0 / width**0.5)
        scale[i * rows : (i + 1) * rows] = jnp.broadcast_to(value, (rows, 128))


def upper_kernel(docs, own, after, kept, scale, own_kept, sems):
    last = pltpu.make_async_copy(own, own_kept, sems.at[4])
    last.start()
    take(docs, 0, kept, scale, sems)
    last.wait()


def lower_kernel(docs, after, kept, scale, sems):
    take(docs, kept.shape[0], kept, scale, sems)


def assemble(pieces, ready, z):
    for b, panel in enumerate(ready):
        for x, y, core, piece in pieces:
            for k in range(4):
                for turn in range(2):
                    dz, dx = asked_of(turn, y, core)
                    start = (z ^ k ^ dz) * 32 + (x ^ dx) * 16
                    rows = pl.ds(pl.multiple_of(start, 16), 16)
                    start = pl.multiple_of((z ^ k) * 128, 128)
                    panel[rows, pl.ds(start, 128)] = piece[
                        k, turn * 16 : (turn + 1) * 16, b * 128 : (b + 1) * 128
                    ]


def columns(docs, at, rows, side, b):
    parts = []
    for block in range(b * 4, b * 4 + 4):
        start = pl.multiple_of(block * 256 + side * 128, 128)
        parts.append(docs[pl.ds(at, rows), pl.ds(start, 128)])
    return jnp.concatenate(parts, axis=1)


def product(docs, at, rows, side, ready):
    total = times(columns(docs, at, rows, side, 0), ready[0][...])
    for b in range(1, len(ready)):
        total += times(columns(docs, at, rows, side, b), ready[b][...])
    return total


def times(left, right):
    return lax.dot_general(left, right, (((1,), (1,)), ((), ())), preferred_element_type=F32)


def near_kernel(upper, lower, own, own_c, across, across_c, out, *ready):
    y, z, x, c = place()
    assemble(
        ((x, y, c, own), (x, y, 1 - c, own_c), (x, 1 - y, c, across), (x, 1 - y, 1 - c, across_c)),
        ready,
        z,
    )
    count, rows = upper.shape[0], 512
    for half, docs in enumerate((upper, lower)):
        for at in range(0, count, rows):
            out[half * count + at : half * count + at + rows] = product(docs, at, rows, x, ready)


def far_kernel(
    upper,
    lower,
    upper_scale,
    lower_scale,
    near,
    diagonal,
    diagonal_c,
    beside,
    beside_c,
    out,
    made,
    sems,
    *ready,
):
    y, z, x, c = place()
    assemble(
        (
            (1 - x, 1 - y, c, diagonal),
            (1 - x, 1 - y, 1 - c, diagonal_c),
            (1 - x, y, c, beside),
            (1 - x, y, 1 - c, beside_c),
        ),
        ready,
        z,
    )
    count, rows = upper.shape[0], 256
    copies = []
    for half, (docs, scale) in enumerate(((upper, upper_scale), (lower, lower_scale))):
        for at in range(0, count, rows):
            here = half * count + at
            got = product(docs, at, rows, 1 - x, ready)
            made[here : here + rows] = (near[here : here + rows] + got) * scale[at : at + rows]
            copies.append(
                pltpu.make_async_copy(
                    made.at[pl.ds(here, rows)], out.at[pl.ds(here, rows)], sems.at[len(copies)]
                )
            )
            copies[-1].start()
    for copy in copies:
        copy.wait()


def in_hbm(array):
    return pltpu.with_memory_space_constraint(array, pltpu.HBM)


def call(kernel, inputs, specs, outs, out_specs, scratch, flops, moved_bytes, limit):
    return pl.pallas_call(
        kernel,
        out_shape=outs,
        in_specs=specs,
        out_specs=out_specs,
        scratch_shapes=scratch,
        cost_estimate=pl.CostEstimate(flops=flops, bytes_accessed=moved_bytes, transcendentals=0),
        compiler_params=pltpu.CompilerParams(vmem_limit_bytes=limit),
    )(*inputs)


def grouped(documents, queries, precond):
    count, width = documents.shape
    vmem, anywhere = pl.BlockSpec(memory_space=pltpu.VMEM), pl.BlockSpec(memory_space=pltpu.HBM)
    like = jax.ShapeDtypeStruct
    mib = 1024 * 1024

    paired = over_core(queries)
    both = jnp.concatenate([queries, paired], axis=0)
    other = over_core(precond)

    def turned(turn):
        def source(y, z, x, c):
            dz, dx = asked_of(turn, y, c)
            return y, z ^ dz, x ^ dx, c

        return moved(both, source)

    asked = {turn: turned(turn) for turn in (1, 0)}
    half_docs, lanes = like((count // 2, width), BF16), like((count // 2, 128), F32)
    upper, upper_scale, own = call(
        upper_kernel,
        (in_hbm(documents), in_hbm(precond), other),
        [anywhere, anywhere, pl.BlockSpec(memory_space=pl.ANY)],
        (half_docs, lanes, like(precond.shape, BF16)),
        (vmem,) * 3,
        [pltpu.SemaphoreType.DMA((5,))],
        count * width,
        count * width,
        2 * mib,
    )
    piece = call(
        condition_kernel,
        (asked[0], asked[1], own, other),
        [vmem] * 4,
        like((32, 512), BF16),
        vmem,
        [],
        2 * 32 * 512 * 1024,
        mib,
        4 * mib,
    )
    line = jnp.stack([piece] + [moved(piece, lambda y, z, x, c: (y, z ^ k, x, c)) for k in (1, 2, 3)])
    diagonal = moved(line, lambda y, z, x, c: (y ^ 1, z, x ^ 1, c))
    beside = moved(line, lambda y, z, x, c: (y, z, x ^ 1, c))
    across = moved(line, lambda y, z, x, c: (y ^ 1, z, x, c))
    lower, lower_scale = call(
        lower_kernel,
        (in_hbm(documents), line),
        [anywhere, pl.BlockSpec(memory_space=pl.ANY)],
        (half_docs, lanes),
        (vmem,) * 2,
        [pltpu.SemaphoreType.DMA((4,))],
        count * width,
        count * width,
        2 * mib,
    )
    across, lower_scale = lax.optimization_barrier((across, lower_scale))
    line_c, across_c, beside_c, diagonal_c = map(over_core, (line, across, beside, diagonal))
    half = [pltpu.VMEM((128, width // 8), BF16)] * 4
    near = call(
        near_kernel,
        (upper, lower, line, line_c, across, across_c),
        [vmem] * 6,
        like((count, 128), F32),
        vmem,
        half,
        count * width * 128,
        count * width,
        12 * mib,
    )
    return call(
        far_kernel,
        (upper, lower, upper_scale, lower_scale, near, diagonal, diagonal_c, beside, beside_c),
        [vmem] * 9,
        like((count, 128), F32),
        anywhere,
        [pltpu.VMEM((count, 128), F32), pltpu.SemaphoreType.DMA((8,)), *half],
        count * width * 128,
        count * width,
        12 * mib,
    )


def general(documents, queries, precond):
    panels, _, panel_width = precond.shape
    width = documents.shape[1]
    asked = lax.all_gather(queries, "row", axis=0, tiled=True)
    asked = asked.reshape(asked.shape[0], panels, panel_width)
    own = jnp.einsum("qbk,brk->bqr", asked, precond, preferred_element_type=F32).astype(BF16)
    ready = lax.all_gather(own, "row", axis=0)
    ready = ready.transpose(2, 1, 0, 3).reshape(-1, width)
    raw = jnp.dot(documents, ready.T, preferred_element_type=F32)
    dense = documents.astype(F32)
    spread = jnp.sqrt(jnp.mean(dense * dense, axis=1) + 1e-06)
    return raw / (spread[:, None] * jnp.sqrt(F32(width)))


def solution(mesh):
    fits = mesh.shape["shard"] == 2 and mesh.shape["row"] == 16
    placed = (P(AXES, None), P("row", None), P(None, "row", None))
    return jax.shard_map(
        grouped if fits else general,
        mesh=mesh,
        in_specs=placed,
        out_specs=P(AXES, None),
        check_vma=False,
    )
```
